768 devices in a mesh: rep: 64 (over x, y, core), fsdp: 12 (over z).
Axes of the slice: x: 4, y: 8, z: 12, core: 2. Of those that a mesh axis runs over, the one named last changes fastest.
Arguments:
- queries: bfloat16 [98304, 4096], P(('rep', 'fsdp')), may hold values from -18 to 18
- resp_keys: bfloat16 [98304, 512], P(('rep', 'fsdp')), may hold values from -6 to 6
- resp_values: bfloat16 [98304, 512], P(('rep', 'fsdp')), may hold values from -6 to 6
- attn_out: bfloat16 [98304, 4096], P(('rep', 'fsdp')), may hold values from -1.796875 to 1.796875
- out_grad: bfloat16 [98304, 4096], P(('rep', 'fsdp')), may hold values from -24 to 24
- lengths: int32 [768], P(('rep', 'fsdp')), may hold values from 1 to 128, 61440 in all
- prefix_keys: bfloat16 [192, 512], P('fsdp'), may hold values from -18 to 18
- prefix_values: bfloat16 [192, 512], P('fsdp'), may hold values from -6 to 6
Outputs:
- query_grad: bfloat16 [98304, 4096], P(('rep', 'fsdp'))
- key_grad: bfloat16 [98304, 512], P(('rep', 'fsdp'))
- value_grad: bfloat16 [98304, 512], P(('rep', 'fsdp'))
- prefix_key_grad: float32 [192, 512], P('fsdp')
- prefix_value_grad: float32 [192, 512], P('fsdp')
The draws below stay inside these ranges and needn't reach their ends.
Inputs may be any that keep to these rules, and one draw needn't show every extreme that they name: The largest of lengths is exactly 128.
All inputs are finite; a program needn't handle non-finite values. No bound on the sum of `lengths` on one device may be relied on, other than what follows from the above.
Results may differ from the reference program's by a relative error of at most 0.0078.
Values may be sent and summed in bfloat16 or wider, within the bound.
No kernel may reach another device: no remote copies, remote signals or barrier semaphores. Data moves between devices by JAX's collectives and lax.ppermute only.
A program may use at most 32 MiB of HBM per device.

```python
import math
import jax
import jax.numpy as jnp
import numpy as np
from jax import lax

HEAD_DIM = 128
Q_HEADS = 32
KV_HEADS = 4
RESP_DEV = 128
TOKENS = 98304
PREFIX = 192
N_REP = 64
N_FSDP = 12


def draw_queries(key, part):
    drawn = jnp.clip(jax.random.normal(jax.random.fold_in(key, 11), (TOKENS, Q_HEADS * HEAD_DIM), jnp.float32), -6.0, 6.0)
    return drawn.astype(jnp.bfloat16)


def draw_prefix_keys(key, part):
    drawn = jnp.clip(jax.random.normal(jax.random.fold_in(key, 13), (PREFIX, KV_HEADS * HEAD_DIM), jnp.float32), -6.0, 6.0)
    return drawn.astype(jnp.bfloat16)


def block_levels(rng, dims, cuts, smallest, top_value):
    level = 1.0
    for position, parts in cuts:
        draws = jax.random.uniform(jax.random.fold_in(jax.random.fold_in(rng, 6), position), (parts,), jnp.float32, smallest / len(cuts), top_value / len(cuts))
        level = level * jnp.repeat(jnp.exp(draws), dims[position] // parts).reshape((-1,) + (1,) * (len(dims) - 1 - position))
    return level


def profile(count, total, limit, skew):
    loads = [(1 << 20) // math.isqrt(grade ** skew) + 1 for grade in range(2, count + 1)]
    spare, holding = total - limit - (count - 1), [1] * (count - 1)
    while spare > 0:
        candidates = [i for i in range(count - 1) if holding[i] < limit]
        mass, budget = sum([loads[i] for i in candidates]), spare
        for i in candidates:
            more = min(limit - holding[i], max(1, budget * loads[i] // mass), spare)
            holding[i] = holding[i] + more
            spare = spare - more
    return np.array([limit] + holding)


def ragged(stream_key, number_of, total, limit, slope):
    if number_of == 2:
        one = jax.random.randint(stream_key, (), max(1, total - limit), min(limit, total - 1) + 1)
        return jnp.stack([one, total - one])
    sizes = jnp.asarray(profile(number_of, total, limit, slope), jnp.int32)
    twos = (number_of - 1) // 2
    donor, taker = sizes[1:1 + 2 * twos:2], sizes[2:2 + 2 * twos:2]
    margin = jnp.minimum(donor - 1, limit - taker)
    passed = jax.random.randint(jax.random.fold_in(stream_key, 1), (twos,), 0, 1 << 20) % (margin + 1)
    sizes = sizes.at[1:1 + 2 * twos:2].set(donor - passed).at[2:2 + 2 * twos:2].set(taker + passed)
    return sizes[jax.random.permutation(jax.random.fold_in(stream_key, 2), number_of)]


def normal_values(key, extent, scale, reach, cuts=(), held_as=jnp.bfloat16):
    gain = block_levels(key, extent, cuts, -0.22, 0.18) if cuts else 1.0
    result = jax.random.normal(key, extent, jnp.float32) * scale * gain
    return jnp.minimum(jnp.maximum(result, -reach), reach).astype(held_as)


def setup_inputs(seed: int = 0) -> dict:
    splits = jax.random.split(jax.random.key(seed), 9)
    return {
        "queries": draw_queries(jax.random.fold_in(splits[8], 71), 0),
        "resp_keys": normal_values(splits[1], (TOKENS, KV_HEADS * HEAD_DIM), 1.0, 6.0, ((0, 768),)),
        "resp_values": normal_values(splits[2], (TOKENS, KV_HEADS * HEAD_DIM), 1.0, 6.0, ((0, 768),)),
        "attn_out": normal_values(splits[3], (TOKENS, Q_HEADS * HEAD_DIM), 0.3, 1.796875, ((0, 768),)),
        "out_grad": normal_values(splits[4], (TOKENS, Q_HEADS * HEAD_DIM), 4.0, 24.0, ((0, 768),)),
        "lengths": ragged(splits[5], N_REP * N_FSDP, N_REP * N_FSDP * RESP_DEV * 5 // 8, RESP_DEV, 1).astype(jnp.int32),
        "prefix_keys": draw_prefix_keys(jax.random.fold_in(splits[8], 71), 0),
        "prefix_values": normal_values(splits[7], (PREFIX, KV_HEADS * HEAD_DIM), 1.0, 6.0, ((0, 12),)),
    }


masked_fill = -1e30


def rounded(values):
    return lax.optimization_barrier(values.astype(jnp.bfloat16)).astype(jnp.float32)


def device_grads(queries, resp_keys, resp_values, attn_out, out_grad, length, prefix_keys, prefix_values):
    resp_rows = queries.shape[0]
    prefix_rows = prefix_keys.shape[0]
    key_count = prefix_rows + resp_rows
    all_keys = jnp.concatenate([prefix_keys, resp_keys], axis=0)
    all_values = jnp.concatenate([prefix_values, resp_values], axis=0)
    row_index = jnp.arange(resp_rows, dtype=jnp.int32)[:, None]
    col_index = jnp.arange(key_count, dtype=jnp.int32)[None, :]
    live_rows = row_index < length
    visible = live_rows & ((col_index < prefix_rows) | (col_index - prefix_rows <= row_index))
    dead_rows = 1.0 - live_rows.astype(jnp.float32)
    group_size = Q_HEADS // KV_HEADS
    score_scale = HEAD_DIM ** -0.5
    block_width = group_size * HEAD_DIM
    query_parts = []
    key_parts = []
    value_parts = []
    for group_index in range(KV_HEADS):
        lower = group_index * block_width
        q_block = queries[:, lower:lower + block_width].reshape(resp_rows, group_size, HEAD_DIM).astype(jnp.float32)
        out_block = attn_out[:, lower:lower + block_width].reshape(resp_rows, group_size, HEAD_DIM).astype(jnp.float32)
        grad_block = out_grad[:, lower:lower + block_width].reshape(resp_rows, group_size, HEAD_DIM).astype(jnp.float32)
        key_block = all_keys[:, group_index * HEAD_DIM:(group_index + 1) * HEAD_DIM].astype(jnp.float32)
        value_block = all_values[:, group_index * HEAD_DIM:(group_index + 1) * HEAD_DIM].astype(jnp.float32)
        scores = jnp.einsum("rhd,kd->hrk", q_block, key_block) * score_scale
        scores = jnp.where(visible[None], scores, masked_fill)
        row_max = jnp.max(scores, axis=2, keepdims=True)
        shifted = jnp.where(visible[None], jnp.exp(scores - row_max), 0.0)
        denominator = jnp.sum(shifted, axis=2, keepdims=True) + dead_rows[None]
        log_total = row_max + jnp.log(denominator)
        attn_prob = jnp.where(visible[None], jnp.exp(scores - log_total), 0.0)
        value_part = jnp.einsum("hrk,rhd->kd", rounded(attn_prob), grad_block)
        prob_grad = jnp.einsum("rhd,kd->hrk", grad_block, value_block)
        row_delta = jnp.einsum("rhd,rhd->hr", grad_block, out_block)
        score_half = rounded(attn_prob * (prob_grad - row_delta[:, :, None]))
        query_part = jnp.einsum("hrk,kd->rhd", score_half, key_block) * score_scale
        key_part = jnp.einsum("hrk,rhd->kd", score_half, q_block) * score_scale
        query_parts.append(query_part.reshape(resp_rows, block_width))
        key_parts.append(key_part)
        value_parts.append(value_part)
    query_grad = jnp.concatenate(query_parts, axis=1).astype(jnp.bfloat16)
    key_whole = jnp.concatenate(key_parts, axis=1)
    value_whole = jnp.concatenate(value_parts, axis=1)
    return (query_grad, key_whole[prefix_rows:].astype(jnp.bfloat16), value_whole[prefix_rows:].astype(jnp.bfloat16),
            key_whole[:prefix_rows], value_whole[:prefix_rows])


def reference(queries, resp_keys, resp_values, attn_out, out_grad, lengths, prefix_keys, prefix_values):
    device_count = N_REP * N_FSDP

    def split_rows(array):
        return array.reshape(device_count, RESP_DEV, array.shape[1])

    def device_step(carried, pieces):
        query_dev, key_dev, value_dev, out_dev, grad_dev, length = pieces
        results = device_grads(query_dev, key_dev, value_dev, out_dev, grad_dev, length, prefix_keys, prefix_values)
        return (carried[0] + results[3], carried[1] + results[4]), (results[0], results[1], results[2])

    zero_sums = jnp.zeros((PREFIX, KV_HEADS * HEAD_DIM), jnp.float32)
    sums, grads = lax.scan(device_step, (zero_sums, zero_sums),
                           (split_rows(queries), split_rows(resp_keys), split_rows(resp_values),
                            split_rows(attn_out), split_rows(out_grad), lengths))
    return (grads[0].reshape(TOKENS, Q_HEADS * HEAD_DIM), grads[1].reshape(TOKENS, KV_HEADS * HEAD_DIM),
            grads[2].reshape(TOKENS, KV_HEADS * HEAD_DIM), sums[0], sums[1])
```

```python
import functools

import jax
import jax.numpy as jnp
from jax import lax
from jax.experimental import pallas as pl
from jax.experimental.pallas import tpu as pltpu
from jax.sharding import Mesh, PartitionSpec as P

HEAD_DIM = 128
Q_HEADS = 32
KV_HEADS = 4
GROUP = Q_HEADS // KV_HEADS
PAIR = 2

bf16 = jnp.bfloat16
f32 = jnp.float32
SCALE = HEAD_DIM ** (-0.5)
LOG2E = 1.4426950408889634
masked_fill = -1e30


def dot(a, b, ca, cb):
    return lax.dot_general(a, b, (((ca,), (cb,)), ((), ())), preferred_element_type=f32)


def grads_kernel(
    meta, q_ref, do_ref, o_ref, k_ref, v_ref, pk_ref, pv_ref,
    dq_ref, dk_ref, dv_ref, pdk_ref, pdv_ref, p_s, s_s,
):
    rows = q_ref.shape[0]
    prefix = pk_ref.shape[0]
    length = meta[0]
    keys = jnp.concatenate([pk_ref[...], k_ref[...]], axis=0)
    values = jnp.concatenate([pv_ref[...], v_ref[...]], axis=0)
    key_count = prefix + rows
    eye = (
        lax.broadcasted_iota(jnp.int32, (HEAD_DIM, HEAD_DIM), 0)
        == lax.broadcasted_iota(jnp.int32, (HEAD_DIM, HEAD_DIM), 1)
    ).astype(f32).astype(bf16)
    keys_t = dot(eye, keys, 1, 1).astype(bf16)
    wide = PAIR * rows
    time = lax.broadcasted_iota(jnp.int32, (1, wide), 1) % rows
    live = time < length
    own = lax.broadcasted_iota(jnp.int32, (rows, wide), 0)
    causal = own <= lax.broadcasted_iota(jnp.int32, (rows, wide), 1) % rows
    ones = jnp.ones((8, 2 * HEAD_DIM), bf16)

    def stacked(ref, first, count):
        return jnp.concatenate(
            [ref[:, h * HEAD_DIM : (h + 1) * HEAD_DIM] for h in range(first, first + count)], axis=0
        )

    for pair in range(GROUP // PAIR):
        first = pair * PAIR
        q = stacked(q_ref, first, PAIR)
        grad = stacked(do_ref, first, PAIR)
        out = stacked(o_ref, first, PAIR)
        prod = grad.astype(f32) * out.astype(f32)
        high = prod.astype(bf16)
        low = (prod - high.astype(f32)).astype(bf16)
        delta = dot(ones, jnp.concatenate([high, low], axis=1), 1, 1)[0:1]
        scores = dot(keys, q, 1, 1)
        s_p = scores[:prefix]
        s_r = jnp.where(causal, scores[prefix:], masked_fill)
        top = jnp.maximum(
            jnp.max(s_p, axis=0, keepdims=True), jnp.max(s_r, axis=0, keepdims=True)
        )
        e_p = jnp.exp2((s_p - top) * (SCALE * LOG2E))
        e_r = jnp.exp2((s_r - top) * (SCALE * LOG2E))
        total = jnp.sum(e_p, axis=0, keepdims=True) + jnp.sum(e_r, axis=0, keepdims=True)
        weight = jnp.where(live, 1.0 / total, 0.0)
        prob = jnp.concatenate([e_p, e_r], axis=0) * weight
        prob_grad = dot(values, grad, 1, 1)
        score_half = (prob * (prob_grad - delta)).astype(bf16)
        p_s[:, first * rows : (first + PAIR) * rows] = prob.astype(bf16)
        s_s[:, first * rows : (first + PAIR) * rows] = score_half
        dq_t = dot(keys_t, score_half, 1, 0) * SCALE
        for i in range(PAIR):
            lo = (first + i) * HEAD_DIM
            dq_ref[:, lo : lo + HEAD_DIM] = dq_t[:, i * rows : (i + 1) * rows].T.astype(bf16)
    dv = dot(p_s[...], stacked(do_ref, 0, GROUP), 1, 0)
    dk = dot(s_s[...], stacked(q_ref, 0, GROUP), 1, 0) * SCALE
    dk_ref[...] = dk[prefix:].astype(bf16)
    dv_ref[...] = dv[prefix:].astype(bf16)
    pdk_ref[...] = dk[:prefix]
    pdv_ref[...] = dv[:prefix]


def local_grads(length, queries, out_grad, attn_out, keys, values, prefix_keys, prefix_values):
    rows = queries.shape[0]
    prefix = prefix_keys.shape[0]
    block = GROUP * HEAD_DIM
    wide = pl.BlockSpec((rows, block), lambda g, m: (0, g))
    slim = pl.BlockSpec((rows, HEAD_DIM), lambda g, m: (0, g))
    pre = pl.BlockSpec((prefix, HEAD_DIM), lambda g, m: (0, g))
    return pl.pallas_call(
        grads_kernel,
        grid_spec=pltpu.PrefetchScalarGridSpec(
            num_scalar_prefetch=1,
            grid=(KV_HEADS,),
            in_specs=[wide, wide, wide, slim, slim, pre, pre],
            out_specs=[wide, slim, slim, pre, pre],
            scratch_shapes=[
                pltpu.VMEM((prefix + rows, GROUP * rows), bf16),
                pltpu.VMEM((prefix + rows, GROUP * rows), bf16),
            ],
        ),
        out_shape=[
            jax.ShapeDtypeStruct((rows, Q_HEADS * HEAD_DIM), bf16),
            jax.ShapeDtypeStruct((rows, KV_HEADS * HEAD_DIM), bf16),
            jax.ShapeDtypeStruct((rows, KV_HEADS * HEAD_DIM), bf16),
            jax.ShapeDtypeStruct((prefix, KV_HEADS * HEAD_DIM), f32),
            jax.ShapeDtypeStruct((prefix, KV_HEADS * HEAD_DIM), f32),
        ],
        compiler_params=pltpu.CompilerParams(vmem_limit_bytes=32 * 1024 * 1024),
        name="grads",
    )(length, queries, out_grad, attn_out, keys, values, prefix_keys, prefix_values)


def exchanged(x, axes):
    return lax.all_to_all(x, axes, 0, 0, tiled=True)


def on_device(
    queries, resp_keys, resp_values, attn_out, out_grad, lengths, prefix_keys, prefix_values
):
    core = lax.axis_index("core")
    n_x, n_y, n_z = lax.axis_size("x"), lax.axis_size("y"), lax.axis_size("z")
    part = prefix_keys.shape[0]
    width = prefix_keys.shape[1]
    mine = jnp.where(core == 0, prefix_keys, prefix_values)
    rows = exchanged(jnp.broadcast_to(mine[None], (n_z, part, width)), "z")
    both = lax.all_gather(rows.reshape(n_z * part, width), "core")
    query_grad, key_grad, value_grad, pre_k, pre_v = local_grads(
        lengths, queries, out_grad, attn_out, resp_keys, resp_values, both[0], both[1]
    )
    theirs = jnp.where(core == 0, pre_v, pre_k).astype(bf16)
    keep = jnp.where(core == 0, pre_k, pre_v)
    got = lax.ppermute(theirs, "core", [(0, 1), (1, 0)])
    chip = (keep + got.astype(f32)).astype(bf16)
    cols = width // n_x
    blocks = chip.reshape(n_z, part, n_x, cols).transpose(2, 0, 1, 3).reshape(n_x * n_z, part, cols)
    summed = jnp.sum(exchanged(blocks, ("x", "z")).astype(f32), axis=0)
    spread = exchanged(jnp.broadcast_to(summed[None], (n_x * n_y, part, cols)), ("x", "y"))
    whole = jnp.sum(spread.reshape(n_x, n_y, part, cols), axis=1)
    whole = whole.transpose(1, 0, 2).reshape(part, width)
    final = lax.all_gather(whole, "core")
    return (query_grad, key_grad, value_grad, final[0], final[1])


def solution(mesh):
    n_rep, n_z = mesh.devices.shape
    n_y = 8
    chips = Mesh(mesh.devices.reshape(n_rep // (2 * n_y), n_y, 2, n_z), ("x", "y", "core", "z"))
    rep = ("x", "y", "core")
    rows = P((*rep, "z"), None)
    in_specs = (rows, rows, rows, rows, rows, P((*rep, "z")), P("z", None), P("z", None))
    out_specs = (rows, rows, rows, P("z", None), P("z", None))
    return jax.shard_map(
        on_device, mesh=chips, in_specs=in_specs, out_specs=out_specs, check_vma=False
    )
```

```python
import jax
import jax.numpy as jnp
from jax import lax
from jax.experimental import pallas as pl
from jax.experimental.pallas import tpu as pltpu
from jax.sharding import Mesh, PartitionSpec as P

HEAD_DIM = 128
Q_HEADS = 32
KV_HEADS = 4
GROUP = Q_HEADS // KV_HEADS
PAIR = 2
BLOCK = GROUP * HEAD_DIM

bf16 = jnp.bfloat16
f32 = jnp.float32
SCALE = HEAD_DIM ** (-0.5)
EXP2_SCALE = SCALE * 1.4426950408889634
masked_fill = -1e30
VMEM_LIMIT = 24 * 1024 * 1024


def dot(a, b, ca, cb):
    return lax.dot_general(a, b, (((ca,), (cb,)), ((), ())), preferred_element_type=f32)


def stacked(ref, first, count):
    return jnp.concatenate(
        [ref[:, h * HEAD_DIM : (h + 1) * HEAD_DIM] for h in range(first, first + count)], axis=0
    )


def transposed(x):
    side = lax.broadcasted_iota(jnp.int32, (HEAD_DIM, HEAD_DIM), 0)
    eye = (side == lax.broadcasted_iota(jnp.int32, (HEAD_DIM, HEAD_DIM), 1)).astype(f32).astype(bf16)
    return dot(eye, x, 1, 1).astype(bf16)


def own_kernel(q_ref, do_ref, o_ref, k_ref, v_ref, e_ref, g_ref, stat_ref):
    rows = q_ref.shape[0]
    wide = PAIR * rows
    keys, values = k_ref[...], v_ref[...]
    causal = (
        lax.broadcasted_iota(jnp.int32, (rows, wide), 0)
        <= lax.broadcasted_iota(jnp.int32, (rows, wide), 1) % rows
    )
    ones = jnp.ones((8, 2 * HEAD_DIM), bf16)
    for first in range(0, GROUP, PAIR):
        cols = slice(first * rows, (first + PAIR) * rows)
        q, grad, out = (stacked(r, first, PAIR) for r in (q_ref, do_ref, o_ref))
        prod = grad.astype(f32) * out.astype(f32)
        high = prod.astype(bf16)
        low = (prod - high.astype(f32)).astype(bf16)
        delta = dot(ones, jnp.concatenate([high, low], axis=1), 1, 1)
        scores = jnp.where(causal, dot(keys, q, 1, 1), masked_fill)
        top = jnp.max(scores, axis=0, keepdims=True)
        e = jnp.exp2((scores - top) * EXP2_SCALE)
        e_ref[:, cols] = e
        g_ref[:, cols] = e * (dot(values, grad, 1, 1) - delta[0:1])
        stat_ref[0:8, cols] = jnp.broadcast_to(top, (8, wide))
        stat_ref[8:16, cols] = jnp.broadcast_to(jnp.sum(e, axis=0, keepdims=True), (8, wide))
        stat_ref[16:24, cols] = delta


def prefix_kernel(
    meta, q_ref, do_ref, shared_ref, stat_ref, s_out, w_ref, sums_ref, p_s, s_ref, sems
):
    rows = q_ref.shape[0]
    wide = PAIR * rows
    live = lax.broadcasted_iota(jnp.int32, (1, wide), 1) % rows < meta[0]
    copies = []
    for group in range(KV_HEADS):
        slim = slice(group * HEAD_DIM, (group + 1) * HEAD_DIM)
        keys, values = shared_ref[0, :, slim], shared_ref[1, :, slim]
        for first in range(group * GROUP, (group + 1) * GROUP, PAIR):
            cols = slice(first * rows, (first + PAIR) * rows)
            q, grad = (stacked(r, first, PAIR) for r in (q_ref, do_ref))
            own_top, own_sum = stat_ref[0:1, cols], stat_ref[8:9, cols]
            delta = stat_ref[16:17, cols]
            scores = dot(keys, q, 1, 1)
            top = jnp.maximum(jnp.max(scores, axis=0, keepdims=True), own_top)
            e = jnp.exp2((scores - top) * EXP2_SCALE)
            own = jnp.exp2((own_top - top) * EXP2_SCALE)
            total = jnp.sum(e, axis=0, keepdims=True) + own_sum * own
            weight = jnp.where(live, 1.0 / total, 0.0)
            prob = e * weight
            p_s[:, cols] = prob.astype(bf16)
            s_ref[:, cols] = (prob * (dot(values, grad, 1, 1) - delta)).astype(bf16)
            w_ref[:, cols] = jnp.broadcast_to(own * weight, (8, wide))
        cols = slice(group * GROUP * rows, (group + 1) * GROUP * rows)
        copies.append(
            pltpu.make_async_copy(s_ref.at[:, cols], s_out.at[:, cols], sems.at[group])
        )
        copies[-1].start()
        q, grad = (stacked(r, group * GROUP, GROUP) for r in (q_ref, do_ref))
        sums_ref[1, :, slim] = dot(p_s[:, cols], grad, 1, 0).astype(bf16)
        sums_ref[0, :, slim] = (dot(s_ref[:, cols], q, 1, 0) * SCALE).astype(bf16)
    for copy in copies:
        copy.wait()


def rest_kernel(
    q_ref, do_ref, k_ref, pk_ref, e_ref, g_ref, s_ref, w_ref, dq_ref, dk_ref, dv_ref, p_s, s_s
):
    rows = q_ref.shape[0]
    keys_t, prefix_t = transposed(k_ref[...]), transposed(pk_ref[0])
    for first in range(0, GROUP, PAIR):
        cols = slice(first * rows, (first + PAIR) * rows)
        weight = w_ref[0:1, cols]
        p_s[:, cols] = (e_ref[:, cols] * weight).astype(bf16)
        score_half = (g_ref[:, cols] * weight).astype(bf16)
        s_s[:, cols] = score_half
        dq_t = (dot(prefix_t, s_ref[:, cols], 1, 0) + dot(keys_t, score_half, 1, 0)) * SCALE
        for i in range(PAIR):
            lo = (first + i) * HEAD_DIM
            dq_ref[:, lo : lo + HEAD_DIM] = dq_t[:, i * rows : (i + 1) * rows].T.astype(bf16)
    dv_ref[...] = dot(p_s[...], stacked(do_ref, 0, GROUP), 1, 0).astype(bf16)
    dk_ref[...] = (dot(s_s[...], stacked(q_ref, 0, GROUP), 1, 0) * SCALE).astype(bf16)


def columns(rows, width):
    return pl.BlockSpec((rows, width), lambda g, *_: (0, g))


def prefix_columns(which, rows):
    return pl.BlockSpec((1, rows, HEAD_DIM), lambda g, *_: (which, 0, g))


def shape(rows, width, dtype):
    return pltpu.HBM((rows, width), dtype)


def held(*sizes):
    return pltpu.VMEM(sizes[:-1], sizes[-1])


def hbm(*arrays):
    return [pltpu.with_memory_space_constraint(a, pltpu.HBM) for a in arrays]


def vmem(*arrays):
    return [pltpu.with_memory_space_constraint(a, pltpu.VMEM) for a in arrays]


def call(kernel, name, scalars, in_specs, out_specs, out_shape, scratch, flops, moved):
    return pl.pallas_call(
        kernel,
        grid_spec=pltpu.PrefetchScalarGridSpec(
            num_scalar_prefetch=scalars,
            grid=(KV_HEADS,),
            in_specs=in_specs,
            out_specs=out_specs,
            scratch_shapes=scratch,
        ),
        out_shape=out_shape,
        compiler_params=pltpu.CompilerParams(vmem_limit_bytes=VMEM_LIMIT),
        cost_estimate=pl.CostEstimate(flops=flops, bytes_accessed=moved, transcendentals=0),
        name=name,
    )


def own_part(queries, out_grad, attn_out, keys, values):
    rows = queries.shape[0]
    wide, slim = columns(rows, BLOCK), columns(rows, HEAD_DIM)
    total = Q_HEADS * rows
    return call(
        own_kernel, "own_part", 0,
        [wide, wide, wide, slim, slim],
        [columns(rows, GROUP * rows), columns(rows, GROUP * rows), columns(24, GROUP * rows)],
        [shape(rows, total, f32), shape(rows, total, f32), held(24, total, f32)],
        [], 1 << 29, 8 << 20,
    )(*hbm(queries, out_grad, attn_out, keys, values))


def prefix_part(length, queries, out_grad, shared, stats):
    rows, prefix = queries.shape[0], shared.shape[1]
    total = Q_HEADS * rows
    whole = pl.BlockSpec(memory_space=pltpu.VMEM)
    return pl.pallas_call(
        prefix_kernel,
        in_specs=[pl.BlockSpec(memory_space=pltpu.SMEM), whole, whole, whole, whole],
        out_specs=[pl.BlockSpec(memory_space=pltpu.HBM), whole, whole],
        out_shape=[
            shape(prefix, total, bf16), held(8, total, f32),
            held(2, prefix, KV_HEADS * HEAD_DIM, bf16),
        ],
        scratch_shapes=[
            pltpu.VMEM((prefix, total), bf16), pltpu.VMEM((prefix, total), bf16),
            pltpu.SemaphoreType.DMA((KV_HEADS,)),
        ],
        compiler_params=pltpu.CompilerParams(vmem_limit_bytes=VMEM_LIMIT),
        cost_estimate=pl.CostEstimate(flops=1 << 30, bytes_accessed=5 << 20, transcendentals=0),
        name="prefix_part",
    )(length, *vmem(queries, out_grad, shared, stats))


def rest_part(queries, out_grad, keys, shared, e, g, score_half, weight):
    rows, prefix = queries.shape[0], shared.shape[1]
    wide, slim = columns(rows, BLOCK), columns(rows, HEAD_DIM)
    heads = columns(rows, GROUP * rows)
    return call(
        rest_kernel, "rest_part", 0,
        [
            wide, wide, slim, prefix_columns(0, prefix), heads, heads,
            columns(prefix, GROUP * rows), columns(8, GROUP * rows),
        ],
        [wide, slim, slim],
        [
            shape(rows, Q_HEADS * HEAD_DIM, bf16), shape(rows, KV_HEADS * HEAD_DIM, bf16),
            shape(rows, KV_HEADS * HEAD_DIM, bf16),
        ],
        [pltpu.VMEM((rows, GROUP * rows), bf16), pltpu.VMEM((rows, GROUP * rows), bf16)],
        1 << 29, 9 << 20,
    )(*vmem(queries, out_grad), *hbm(keys), shared, *hbm(e, g, score_half), weight)


def exchanged(x, axes):
    return lax.all_to_all(x, axes, 0, 0, tiled=True)


def on_device(
    queries, resp_keys, resp_values, attn_out, out_grad, lengths, prefix_keys, prefix_values
):
    core = lax.axis_index("core")
    n_x, n_y, n_z = lax.axis_size("x"), lax.axis_size("y"), lax.axis_size("z")
    part, width = prefix_keys.shape
    mine = jnp.where(core == 0, prefix_keys, prefix_values)
    rows = exchanged(jnp.broadcast_to(mine[None], (n_z, part, width)), "z")
    e, g, stats = own_part(queries, out_grad, attn_out, resp_keys, resp_values)
    shared = lax.all_gather(rows.reshape(n_z * part, width), "core")
    score_half, weight, sums = prefix_part(lengths, queries, out_grad, shared, stats)
    both = lax.all_gather(sums, "core")
    halves = [jnp.where(core == 0, both[i, 0], both[i, 1]).astype(f32) for i in range(2)]
    chip = (halves[0] + halves[1]).astype(bf16)
    chip, score_half = lax.optimization_barrier((chip, score_half))
    cols = width // n_x
    blocks = chip.reshape(n_z, part, n_x, cols).transpose(2, 0, 1, 3).reshape(n_x * n_z, part, cols)
    blocks = exchanged(blocks, ("x", "z"))
    query_grad, key_grad, value_grad = rest_part(
        queries, out_grad, resp_keys, shared, e, g, score_half, weight
    )
    summed = jnp.sum(blocks.astype(f32), axis=0).astype(bf16)
    spread = exchanged(jnp.broadcast_to(summed[None], (n_x * n_y, part, cols)), ("x", "y"))
    whole = jnp.sum(spread.reshape(n_x, n_y, part, cols).astype(f32), axis=1)
    final = lax.all_gather(whole.transpose(1, 0, 2).reshape(part, width), "core")
    return (query_grad, key_grad, value_grad, final[0], final[1])


def solution(mesh):
    n_rep, n_z = mesh.devices.shape
    n_y = 8
    chips = Mesh(mesh.devices.reshape(n_rep // (2 * n_y), n_y, 2, n_z), ("x", "y", "core", "z"))
    rep = ("x", "y", "core")
    rows = P((*rep, "z"), None)
    in_specs = (rows, rows, rows, rows, rows, P((*rep, "z")), P("z", None), P("z", None))
    out_specs = (rows, rows, rows, P("z", None), P("z", None))
    return jax.shard_map(
        on_device, mesh=chips, in_specs=in_specs, out_specs=out_specs, check_vma=False
    )
```
